256 devices in a mesh: dp: 32 (over z, y), mp: 8 (over x, core).
Axes of the slice: x: 4, y: 4, z: 8, core: 2. Of those that a mesh axis runs over, the one named last changes fastest.
Arguments:
- queries_vec: bfloat16 [128, 64, 2048], P('dp', None, 'mp')
- retr_query: bfloat16 [128, 4096], P('dp', 'mp'), may hold values from -6 to 6
- passages: bfloat16 [256, 64, 4096], P('dp', None, 'mp'), may hold values from -6 to 6
- kv_weight: bfloat16 [4096, 2, 2048], P(None, None, 'mp'), may hold values from -0.09375 to 0.09375
- retrieval: int32 [128, 8], replicated, may hold values from 0 to 255, as said below
- lengths: int32 [256], replicated, may hold values from 8 to 64, as said below
- ctx_cot: bfloat16 [128, 64, 2048], P('dp', None, 'mp'), may hold values from -6 to 6
Outputs:
- context: bfloat16 [128, 64, 2048], P('dp', None, 'mp')
- divergence: float32 [128], P('dp')
- grad_passages: bfloat16 [256, 64, 4096], P('dp', None, 'mp')
The draws below stay inside these ranges and needn't reach their ends.
Inputs may be any that keep to these rules, and one draw needn't show every extreme that they name: `retrieval`: each query's 8 ids differ; within the 4 queries of one index of dp (aligned blocks of 4 rows) no id repeats, and at most 2 of their ids share an owner (id // 8), exactly 2 for some owner in every block. `lengths`: multiples of 8.
All inputs are finite; a program needn't handle non-finite values.
Results may differ from the reference program's by a relative error of at most 0.015.
Values may be sent and summed in bfloat16 or wider, within the bound.
No kernel may reach another device: no remote copies, remote signals or barrier semaphores. Data moves between devices by JAX's collectives and lax.ppermute only.
A program may use at most 64 MiB of HBM per device.

```python
import jax
import jax.numpy as jnp
from jax import lax

D = 4096
HEADS = 32
HD = 64
PT = 64
LB = 8
K = 8
QT = 64
Q_DEV = 4
P_DEV = 8
CAP = 2
QUERIES = 128
PASSAGES = 256
N_DP = 32


def draw_retrieval(key, part):
    key = jax.random.fold_in(key, 11)
    group_rows = Q_DEV * K
    slot_total = N_DP * CAP
    owner_base = jnp.arange(slot_total, dtype=jnp.int32) // CAP

    def one_group(group_key):
        key_hot, key_order, key_shuffle, key_table = jax.random.split(group_key, 4)
        hot_owner = jax.random.randint(key_hot, (), 0, N_DP)
        order = jax.random.permutation(key_order, slot_total).astype(jnp.int32)
        priority = jnp.where(owner_base == hot_owner, jnp.arange(slot_total, dtype=jnp.int32) - slot_total, order)
        chosen = owner_base[jnp.argsort(priority)][:group_rows]
        chosen = chosen[jax.random.permutation(key_shuffle, group_rows)]
        row_index = jnp.arange(group_rows, dtype=jnp.int32)
        earlier = row_index[:, None] > row_index[None, :]
        ranks = jnp.sum((chosen[:, None] == chosen[None, :]) & earlier, axis=1).astype(jnp.int32)
        noise = jax.random.randint(key_table, (N_DP, P_DEV), 0, 1 << 20) * P_DEV + jnp.arange(P_DEV, dtype=jnp.int32)[None, :]
        table = jnp.argsort(noise, axis=1).astype(jnp.int32)
        return chosen * P_DEV + table[chosen, ranks]
    group_keys = jax.random.split(key, N_DP)
    return jax.vmap(one_group)(group_keys).reshape(N_DP * Q_DEV, K).astype(jnp.int32)


def draw_lengths(key, part):
    key = jax.random.fold_in(key, 23)
    blocks = jax.random.randint(key, (PASSAGES,), 1, 9)
    return (blocks * LB).at[0].set(PT).astype(jnp.int32)


def head_scaled(base, low, high):
    head_of = jnp.arange(HEADS * HD, dtype=jnp.int32) // HD
    ratio = head_of.astype(jnp.float32) / max(HEADS - 1, 1)
    factor = low * (high / low) ** ratio
    return base * factor[None, None, :]


def draw_queries_vec(key, part):
    key = jax.random.fold_in(key, 37)
    shape = (QUERIES, QT, HEADS * HD)
    base = jnp.clip(jax.random.normal(key, shape, jnp.float32), -6.0, 6.0)
    values = head_scaled(base, 0.3, 3.0)
    return values.astype(jnp.bfloat16)


def shard_levels(stream_key, dims, cuts, smallest, largest):
    factor_of, own = 1.0, jax.random.fold_in(stream_key, 6)
    for position, blocks in cuts:
        draws = jnp.exp(jax.random.uniform(jax.random.fold_in(own, position), (blocks,), jnp.float32, smallest / len(cuts), largest / len(cuts)))
        factor_of = factor_of * jnp.repeat(draws, dims[position] // blocks).reshape([-1 if axis == position else 1 for axis in range(len(dims))])
    return factor_of


def normal_values(own_key, dims, spread, limit, cuts=(), held_as=jnp.bfloat16):
    level = shard_levels(own_key, dims, cuts, -0.22, 0.18) if cuts else 1.0
    entries = jax.random.normal(own_key, dims, jnp.float32) * spread * level
    return jnp.minimum(jnp.maximum(entries, -limit), limit).astype(held_as)


def setup_inputs(seed: int = 0) -> dict:
    key_of = jax.random.split(jax.random.key(seed), 8)
    return {
        "queries_vec": draw_queries_vec(jax.random.fold_in(key_of[7], 71), 0),
        "retr_query": normal_values(key_of[1], (QUERIES, D), 1.0, 6.0, ((0, 32), (1, 8))),
        "passages": normal_values(key_of[2], (PASSAGES, PT, D), 1.0, 6.0, ((0, 32), (2, 8))),
        "kv_weight": normal_values(key_of[3], (D, 2, HEADS * HD), D ** -0.5, 0.09375, ((2, 8),)),
        "retrieval": draw_retrieval(jax.random.fold_in(key_of[7], 71), 0),
        "lengths": draw_lengths(jax.random.fold_in(key_of[7], 71), 0),
        "ctx_cot": normal_values(key_of[6], (QUERIES, QT, HEADS * HD), 1.0, 6.0, ((0, 32), (2, 8))),
    }


INV_TEMP = 8.0
DISTILL = 128.0


def reference(queries_vec, retr_query, passages, kv_weight, retrieval, lengths, ctx_cot):
    score_scale = HD ** -0.5
    width_scale = INV_TEMP * D ** -0.5
    weight_flat = kv_weight.reshape(D, 2 * HEADS * HD)
    projected = jnp.dot(passages.reshape(PASSAGES * PT, D), weight_flat, preferred_element_type=jnp.float32)
    projected = projected.astype(jnp.bfloat16).reshape(PASSAGES, PT, 2, HEADS, HD)
    positions = jnp.arange(PT, dtype=jnp.int32)
    valid = (positions[None, :] < lengths[:, None]).astype(jnp.float32)
    length_f = lengths.astype(jnp.float32)
    pooled = (jnp.einsum("pt,ptd->pd", valid, passages.astype(jnp.float32)) / length_f[:, None]).astype(jnp.bfloat16)

    def one_query(carry, inputs):
        grad_rows, grad_pool = carry
        query_vec, retr_vec, picked, cotangent = inputs
        chosen = projected[picked]
        key_mask = valid[picked].reshape(K * PT)
        key_heads = chosen[:, :, 0].reshape(K * PT, HEADS, HD).astype(jnp.float32)
        value_heads = chosen[:, :, 1].reshape(K * PT, HEADS, HD).astype(jnp.float32)
        query_f = query_vec.reshape(QT, HEADS, HD).astype(jnp.float32)
        scores = jnp.einsum("ihd,jhd->hij", query_f, key_heads) * score_scale
        expd = jnp.exp(scores) * key_mask[None, None, :]
        prob = expd / jnp.sum(expd, axis=2, keepdims=True)
        prob_b = prob.astype(jnp.bfloat16)
        ctx_out = jnp.einsum("hij,jhd->ihd", prob_b.astype(jnp.float32), value_heads)
        ctx_out = ctx_out.astype(jnp.bfloat16).reshape(QT, HEADS * HD)
        mass = jnp.sum(prob.reshape(HEADS, QT, K, PT), axis=(0, 1, 3)) / (HEADS * QT)
        retr_score = jnp.dot(pooled[picked], retr_vec, preferred_element_type=jnp.float32) * width_scale
        log_prob = retr_score - jnp.log(jnp.sum(jnp.exp(retr_score)))
        loss_value = jnp.sum(mass * (jnp.log(mass) - log_prob))
        d_score = DISTILL * (jnp.exp(log_prob) - mass)
        pool_grad = ((d_score * width_scale)[:, None] * retr_vec.astype(jnp.float32)[None, :]).astype(jnp.bfloat16)
        cot_f = cotangent.reshape(QT, HEADS, HD).astype(jnp.float32)
        d_prob = jnp.einsum("ihd,jhd->hij", cot_f, value_heads)
        d_scores = prob * (d_prob - jnp.sum(prob * d_prob, axis=2, keepdims=True)) * score_scale
        d_scores_b = d_scores.astype(jnp.bfloat16)
        key_grad = jnp.einsum("hij,ihd->jhd", d_scores_b.astype(jnp.float32), query_f)
        value_grad = jnp.einsum("hij,ihd->jhd", prob_b.astype(jnp.float32), cot_f)
        row_grad = jnp.stack([key_grad.reshape(K, PT, HEADS * HD), value_grad.reshape(K, PT, HEADS * HD)], axis=2)
        row_grad = row_grad.astype(jnp.bfloat16)
        grad_rows = grad_rows.at[picked].add(row_grad.astype(jnp.float32))
        grad_pool = grad_pool.at[picked].add(pool_grad.astype(jnp.float32))
        return (grad_rows, grad_pool), (ctx_out, loss_value)

    start_rows = jnp.zeros((PASSAGES, PT, 2, HEADS * HD), jnp.float32)
    start_pool = jnp.zeros((PASSAGES, D), jnp.float32)
    (grad_rows, grad_pool), (contexts, losses) = lax.scan(
        one_query, (start_rows, start_pool), (queries_vec, retr_query, retrieval, ctx_cot))
    rows_b = grad_rows.astype(jnp.bfloat16).reshape(PASSAGES * PT, 2 * HEADS * HD)
    reader_grad = jnp.dot(rows_b, weight_flat.T, preferred_element_type=jnp.float32).reshape(PASSAGES, PT, D)
    retr_grad = valid[:, :, None] / length_f[:, None, None] * grad_pool[:, None, :]
    grad_passages = (reader_grad + retr_grad).astype(jnp.bfloat16)
    return contexts, losses, grad_passages
```

```python
import jax
import jax.numpy as jnp
from jax import lax
from jax.experimental import pallas as pl
from jax.experimental.pallas import tpu as pltpu
from jax.sharding import Mesh, PartitionSpec as P

HEADS = 32
HD = 64
INV_TEMP = 8.0
DISTILL = 128.0
UNROLL = 4
VMEM_LIMIT = 48 * 1024 * 1024
F32 = jnp.float32
BF16 = jnp.bfloat16
NT = (((1,), (1,)), ((), ()))
TN = (((0,), (0,)), ((), ()))


def shift(x, axis, step):
    size = lax.axis_size(axis)
    return lax.ppermute(x, axis, [(i, (i + step) % size) for i in range(size)])


def swap(x, axis, bit):
    size = lax.axis_size(axis)
    return lax.ppermute(x, axis, [(i, i ^ bit) for i in range(size)])


def head_masks(rows, cols):
    lane = lax.broadcasted_iota(jnp.int32, (rows, cols), 1)
    return [lane // HD == h for h in range(cols // HD)]


def block_diagonal(x, masks):
    zero = jnp.zeros_like(x)
    return jnp.concatenate([jnp.where(m, x, zero) for m in masks], axis=0)


def pair_scores(qb, cb, kv, length, score_scale):
    cols = qb.shape[1]
    scores = lax.dot_general(kv[:, :cols], qb, NT, preferred_element_type=F32) * score_scale
    d_prob = lax.dot_general(kv[:, cols:], cb, NT, preferred_element_type=F32)
    row = lax.broadcasted_iota(jnp.int32, scores.shape, 0)
    return jnp.where(row < length, jnp.exp(scores), 0.0), d_prob


def forward_kernel(count, pair_query, pair_row, pair_len, q_ref, c_ref, kv_ref, sums_ref):
    sums_ref[...] = jnp.zeros_like(sums_ref)
    masks = head_masks(q_ref.shape[1], q_ref.shape[2])
    score_scale = HD ** (-0.5)

    def group(g, carry):
        results = []
        for u in range(UNROLL):
            s = g * UNROLL + u
            qi = pair_query[s]
            qb = block_diagonal(q_ref[qi], masks)
            cb = block_diagonal(c_ref[qi], masks)
            expd, d_prob = pair_scores(qb, cb, kv_ref[pair_row[s]], pair_len[s], score_scale)
            total = jnp.sum(expd, axis=0, keepdims=True)
            safe = jnp.where(total > 0.0, total, 1.0)
            mean = jnp.sum((expd / safe) * d_prob, axis=0, keepdims=True)
            results.append((qi, total, mean))
        for qi, total, mean in results:
            old = sums_ref[qi]
            both = old[:1] + total
            safe = jnp.where(both > 0.0, both, 1.0)
            merged = old[1:] * (old[:1] / safe) + mean * (total / safe)
            sums_ref[qi] = jnp.concatenate([both, merged], axis=0)
        return carry

    lax.fori_loop(0, (count[0] + UNROLL - 1) // UNROLL, group, 0)


def backward_kernel(
    count, pair_query, pair_row, pair_len, q_ref, c_ref, kv_ref, sums_ref,
    dkv_ref, ctx_ref, mass_ref, dkv_acc, ctx_acc,
):
    dkv_acc[...] = jnp.zeros_like(dkv_acc)
    ctx_acc[...] = jnp.zeros_like(ctx_acc)
    mass_ref[...] = jnp.zeros_like(mass_ref)
    cols = q_ref.shape[2]
    masks = head_masks(q_ref.shape[1], cols)
    score_scale = HD ** (-0.5)

    def group(g, carry):
        results = []
        for u in range(UNROLL):
            s = g * UNROLL + u
            qi = pair_query[s]
            row = pair_row[s]
            qb = block_diagonal(q_ref[qi], masks)
            cb = block_diagonal(c_ref[qi], masks)
            kv = kv_ref[row]
            expd, d_prob = pair_scores(qb, cb, kv, pair_len[s], score_scale)
            sums = sums_ref[qi]
            prob = expd / sums[:1]
            prob_b = prob.astype(BF16)
            d_scores = (prob * (d_prob - sums[1:]) * score_scale).astype(BF16)
            key_grad = jnp.dot(d_scores, qb, preferred_element_type=F32)
            value_grad = jnp.dot(prob_b, cb, preferred_element_type=F32)
            full = lax.dot_general(prob_b, kv[:, cols:], TN, preferred_element_type=F32)
            part = jnp.zeros(ctx_acc.shape[1:], F32)
            for h, m in enumerate(masks):
                part = jnp.where(m, full[h * HD : (h + 1) * HD], part)
            results.append((s, qi, row, key_grad, value_grad, part, jnp.sum(prob, axis=0, keepdims=True)))
        for s, qi, row, key_grad, value_grad, part, mass in results:
            dkv_acc[row, :, :cols] += key_grad
            dkv_acc[row, :, cols:] += value_grad
            ctx_acc[qi] += part
            mass_ref[s] = mass
        return carry

    lax.fori_loop(0, (count[0] + UNROLL - 1) // UNROLL, group, 0)
    dkv_ref[...] = dkv_acc[...].astype(BF16)
    ctx_ref[...] = ctx_acc[...].astype(BF16)


def smem():
    return pl.BlockSpec(memory_space=pltpu.SMEM)


def vmem():
    return pl.BlockSpec(memory_space=pltpu.VMEM)


def per_device(queries_vec, retr_query, passages, kv_weight, retrieval, lengths, ctx_cot):
    nz, ny, nx, nc = (lax.axis_size(a) for a in ("z", "y", "x", "core"))
    z, y, x, core = (lax.axis_index(a) for a in ("z", "y", "x", "core"))
    own_count, token_count, local_width = passages.shape
    full_width = kv_weight.shape[0]
    head_cols = kv_weight.shape[2]
    query_count, query_tokens, _ = queries_vec.shape
    picks = retrieval.shape[1]
    width_scale = INV_TEMP * full_width ** (-0.5)
    tokens = own_count * token_count
    kv_cols = 2 * head_cols
    meet_queries = nz * query_count
    meet_rows = ny * own_count
    cap = 2 * nz * ny

    with jax.named_scope("gather_queries"):
        packed = jnp.concatenate(
            [queries_vec, ctx_cot, retr_query.reshape(query_count, -1, head_cols)], axis=1
        )
        met = lax.all_gather(packed, "z", axis=0, tiled=True)
        q_all = met[:, :query_tokens]
        c_all = met[:, query_tokens : 2 * query_tokens]
        rq_all = met[:, 2 * query_tokens :].reshape(meet_queries, local_width)

    with jax.named_scope("project"):
        weight = kv_weight.reshape(full_width, kv_cols)
        blocks = weight.reshape(nx, nc, local_width, kv_cols)

        def weight_block(dx, dc):
            return blocks[(x + dx) % nx, (core + dc) % nc]

        own = passages.reshape(tokens, local_width)
        half = tokens // 2
        left = shift(own, "x", 1)
        right = shift(own, "x", -1)
        own_s = swap(own, "core", 1)
        opp_a = shift(left[:half], "x", 1)
        opp_b = shift(right[half:], "x", -1)
        left_s = swap(left, "core", 1)
        right_s = swap(right, "core", 1)
        opp = jnp.concatenate([opp_a, opp_b], axis=0)
        opp_s = swap(opp, "core", 1)
        acc = jnp.dot(own, weight_block(0, 0), preferred_element_type=F32)
        for part, dx, dc in (
            (own_s, 0, 1), (left, -1, 0), (right, 1, 0), (left_s, -1, 1),
            (right_s, 1, 1), (opp, 2, 0), (opp_s, 2, 1),
        ):
            acc = acc + jnp.dot(part, weight_block(dx, dc), preferred_element_type=F32)
        kv = acc.astype(BF16)

    with jax.named_scope("pool"):
        own_id = z * ny + y
        own_lengths = lax.dynamic_slice_in_dim(lengths, own_id * own_count, own_count)
        positions = jnp.arange(token_count, dtype=jnp.int32)
        own_valid = positions[None, :] < own_lengths[:, None]
        own_len_f = own_lengths.astype(F32)
        pooled = jnp.einsum("pt,ptd->pd", own_valid.astype(BF16), passages, preferred_element_type=F32)
        pooled = (pooled / own_len_f[:, None]).astype(BF16)
        pooled_all = jnp.concatenate([pooled] + [shift(pooled, "y", j) for j in range(1, ny)], axis=0)

    with jax.named_scope("pairs"):
        column = lax.dynamic_index_in_dim(
            retrieval.reshape(nz, ny, query_count, picks), y, axis=1, keepdims=False
        ).reshape(meet_queries * picks)
        flat = jnp.arange(meet_queries * picks, dtype=jnp.int32)
        owner = column // own_count
        chosen = owner // ny == z
        row_of = ((y - owner % ny) % ny) * own_count + column % own_count
        rank = jnp.sum((chosen[None, :] & (flat[None, :] < flat[:, None])).astype(jnp.int32), axis=1)
        slots = jnp.arange(cap, dtype=jnp.int32)
        hot = (rank[None, :] == slots[:, None]) & chosen[None, :]
        pick = lambda v: jnp.sum(jnp.where(hot, v[None, :], 0), axis=1)
        pair_query = pick(flat // picks)
        pair_row = pick(row_of)
        pair_len = pick(lengths[column])
        count = jnp.sum(chosen.astype(jnp.int32)).reshape(1)
        met_rows = jnp.arange(meet_rows, dtype=jnp.int32)
        met_queries = jnp.arange(meet_queries, dtype=jnp.int32)
        dense = (
            (pair_query[:, None, None] == met_queries[None, :, None])
            & (pair_row[:, None, None] == met_rows[None, None, :])
            & (slots < count[0])[:, None, None]
        )
        is_pair = jnp.any(dense, axis=0)

    with jax.named_scope("gather_rows"):
        left = shift(kv, "y", 1)
        right = shift(kv, "y", -1)
        opp_a = shift(left[:half], "y", 1)
        opp_b = shift(right[half:], "y", -1)
        kv_all = jnp.concatenate([kv, left, opp_a, opp_b, right], axis=0)
        kv_all = kv_all.reshape(meet_rows, token_count, kv_cols)

    params = pltpu.CompilerParams(vmem_limit_bytes=VMEM_LIMIT)
    with jax.named_scope("forward"):
        part_sums = pl.pallas_call(
            forward_kernel,
            out_shape=jax.ShapeDtypeStruct((meet_queries, 2, head_cols), F32),
            in_specs=[smem()] * 4 + [vmem()] * 3,
            out_specs=vmem(),
            compiler_params=params,
        )(count, pair_query, pair_row, pair_len, q_all, c_all, kv_all)

    with jax.named_scope("exchange"):
        got = lax.all_to_all(
            part_sums.reshape(nz, query_count, 2, head_cols), "z", split_axis=0, concat_axis=0, tiled=True
        )
        total = jnp.sum(got[:, :, 0], axis=0)
        delta = jnp.sum(got[:, :, 1] * (got[:, :, 0] / total[None]), axis=0)
        mine = jnp.stack([total, delta], axis=1)
        sums = lax.all_to_all(
            jnp.broadcast_to(mine[None], (nz,) + mine.shape), "z", split_axis=0, concat_axis=0, tiled=True
        ).reshape(meet_queries, 2, head_cols)

    with jax.named_scope("backward"):
        dkv, ctx_part, mass_rows = pl.pallas_call(
            backward_kernel,
            out_shape=(
                jax.ShapeDtypeStruct((meet_rows, token_count, kv_cols), BF16),
                jax.ShapeDtypeStruct((meet_queries, query_tokens, head_cols), BF16),
                jax.ShapeDtypeStruct((cap, 1, head_cols), F32),
            ),
            in_specs=[smem()] * 4 + [vmem()] * 4,
            out_specs=(vmem(), vmem(), vmem()),
            scratch_shapes=[
                pltpu.VMEM((meet_rows, token_count, kv_cols), F32),
                pltpu.VMEM((meet_queries, query_tokens, head_cols), F32),
            ],
            compiler_params=params,
        )(count, pair_query, pair_row, pair_len, q_all, c_all, kv_all, sums)

    with jax.named_scope("context"):
        context = lax.psum_scatter(ctx_part, "z", scatter_dimension=0, tiled=True)

    with jax.named_scope("return_rows"):
        p0, p3, p2, p1 = (dkv[j * own_count : (j + 1) * own_count].reshape(tokens, kv_cols) for j in range(ny))
        got_a = shift(p2[:half], "y", 1)
        got_b = shift(p2[half:], "y", -1)
        up = jnp.concatenate([p1[:half] + got_a, p1[half:]], axis=0)
        down = jnp.concatenate([p3[:half], p3[half:] + got_b], axis=0)
        got_u = shift(up, "y", 1)
        got_d = shift(down, "y", -1)
        grad_rows = (p0.astype(F32) + got_u.astype(F32) + got_d.astype(F32)).astype(BF16)

    with jax.named_scope("weights_back"):
        def block(dx, dc):
            return lax.dot_general(grad_rows, weight_block(dx, dc), NT, preferred_element_type=F32)

        def both_cores(dx):
            other = swap(block(dx, 1).astype(BF16), "core", 1)
            return block(dx, 0), other

        m2, o2 = both_cores(2)
        s2 = (m2 + o2.astype(F32)).astype(BF16)
        far_a = shift(s2[:half], "x", 1)
        far_b = shift(s2[half:], "x", -1)
        m1, o1 = both_cores(1)
        s1 = m1 + o1.astype(F32)
        m3, o3 = both_cores(-1)
        s3 = m3 + o3.astype(F32)
        m0, o0 = both_cores(0)
        up = jnp.concatenate([s1[:half] + far_a.astype(F32), s1[half:]], axis=0).astype(BF16)
        down = jnp.concatenate([s3[:half], s3[half:] + far_b.astype(F32)], axis=0).astype(BF16)
        got_u = shift(up, "x", 1)
        got_d = shift(down, "x", -1)
        reader_grad = m0 + o0.astype(F32) + got_u.astype(F32) + got_d.astype(F32)

    with jax.named_scope("distill"):
        score_part = jnp.einsum("qd,pd->qp", rq_all, pooled_all, preferred_element_type=F32)
        mass_pair = jnp.sum(mass_rows, axis=(1, 2))
        mass_part = jnp.sum(jnp.where(dense, mass_pair[:, None, None], 0.0), axis=0)
        both = jnp.stack([score_part, mass_part])
        both = both + swap(both, "core", 1)
        both = both + swap(both, "x", 1)
        both = both + swap(both, "x", 2)
        score = both[0] * width_scale
        mass = both[1] / (HEADS * query_tokens)
        log_mass = jnp.log(jnp.where(is_pair, mass, 1.0))
        stats = jnp.stack([
            jnp.sum(jnp.where(is_pair, jnp.exp(score), 0.0), axis=1),
            jnp.sum(jnp.where(is_pair, mass * (log_mass - score), 0.0), axis=1),
            jnp.sum(jnp.where(is_pair, mass, 0.0), axis=1),
        ])
        for bit in (1, 2, 4):
            stats = stats + swap(stats, "z", bit)
        log_total = jnp.log(stats[0])
        divergence = lax.dynamic_slice_in_dim(stats[1] + log_total * stats[2], z * query_count, query_count)
        d_score = DISTILL * (jnp.exp(score - log_total[:, None]) - mass)
        d_score = jnp.where(is_pair, d_score * width_scale, 0.0)
        pool_part = jnp.einsum(
            "qp,qd->pd", d_score, rq_all.astype(F32), precision=lax.Precision.HIGHEST,
            preferred_element_type=F32,
        ).reshape(ny, own_count, local_width)
        grad_pool = pool_part[0]
        for j in range(1, ny):
            grad_pool = grad_pool + shift(pool_part[j], "y", -j)
        retr_grad = own_valid.astype(F32)[:, :, None] / own_len_f[:, None, None] * grad_pool[:, None, :]

    grad_passages = (reader_grad.reshape(passages.shape) + retr_grad).astype(BF16)
    return (context, divergence, grad_passages)


def solution(mesh):
    grid = Mesh(mesh.devices.reshape(8, 4, 4, 2), ("z", "y", "x", "core"))
    dp, mp = ("z", "y"), ("x", "core")
    in_specs = (
        P(dp, None, mp),
        P(dp, mp),
        P(dp, None, mp),
        P(None, None, mp),
        P(),
        P(),
        P(dp, None, mp),
    )
    out_specs = (P(dp, None, mp), P(dp), P(dp, None, mp))
    return jax.shard_map(
        per_device, mesh=grid, in_specs=in_specs, out_specs=out_specs, check_vma=False
    )
```

```python
import functools

import jax
import jax.numpy as jnp
from jax import lax
from jax.experimental import pallas as pl
from jax.experimental.pallas import tpu as pltpu
from jax.sharding import Mesh, PartitionSpec as P

HEADS = 32
HD = 64
INV_TEMP = 8.0
DISTILL = 128.0
UNROLL = 4
VMEM_LIMIT = 24 * 1024 * 1024
F32 = jnp.float32
BF16 = jnp.bfloat16
NT = (((1,), (1,)), ((), ()))
TN = (((0,), (0,)), ((), ()))


def shift(x, axis, step):
    size = lax.axis_size(axis)
    return lax.ppermute(x, axis, [(i, (i + step) % size) for i in range(size)])


def swap(x, axis, bit):
    size = lax.axis_size(axis)
    return lax.ppermute(x, axis, [(i, i ^ bit) for i in range(size)])


def head_masks(rows, cols):
    lane = lax.broadcasted_iota(jnp.int32, (rows, cols), 1)
    return [lane // HD == h for h in range(cols // HD)]


def block_diagonal(x, masks):
    zero = jnp.zeros_like(x)
    return jnp.concatenate([jnp.where(m, x, zero) for m in masks], axis=0)


def pair_scores(qb, cb, key, value, length):
    scores = lax.dot_general(key, qb, NT, preferred_element_type=F32) * HD ** (-0.5)
    d_prob = lax.dot_general(value, cb, NT, preferred_element_type=F32)
    row = lax.broadcasted_iota(jnp.int32, scores.shape, 0)
    return jnp.where(row < length, jnp.exp(scores), 0.0), d_prob


def load_pair(slot, pair_query, met_ref, masks):
    tokens = masks[0].shape[0]
    both = met_ref[pair_query[slot], : 2 * tokens]
    return block_diagonal(both[:tokens], masks), block_diagonal(both[tokens:], masks)


def join_halves(refs, scratch, sems):
    half = refs[0].shape[0]
    copies = [
        pltpu.make_async_copy(ref, scratch.at[k // 2, pl.ds((k % 2) * half, half)], sems.at[k])
        for k, ref in enumerate(refs)
    ]
    for copy in copies:
        copy.start()
    return copies


def rows_at(row, tokens):
    return pl.ds(pl.multiple_of(row * tokens, tokens), tokens)


def each_group(count, stages, body):
    for i, stage in enumerate(stages):
        groups = (count[stage] + UNROLL - 1) // UNROLL
        lax.fori_loop(0, groups, lambda g, carry: body(g, carry, i, stage), 0)


def row_of(ref, part, index):
    return ref[part, pl.ds(index, 1), :]


def forward_kernel(stages, tokens, last, count, pair_query, pair_row, pair_len, met_ref, *refs):
    n = len(stages)
    kv_refs, refs = refs[: 2 * n], refs[2 * n :]
    out_ref, rows_ref, kv, sems = refs[-4:]
    sums = out_ref.at[0] if last else out_ref
    queries = met_ref.shape[0]
    copies = join_halves(kv_refs, kv, sems)
    rows_ref[...] = jnp.zeros_like(rows_ref)
    if stages[0]:
        sums[:, :queries] = refs[0][...]
    else:
        sums[...] = jnp.zeros(sums.shape, F32)
    if last:
        sums[:, queries:] = jnp.zeros((2, sums.shape[1] - queries, sums.shape[2]), F32)
        sums[0, queries : queries + 1, : refs[1].shape[1]] = refs[1][...]
    slots = rows_ref.shape[0] // n
    cols = kv.shape[-1] // 2
    masks = head_masks(tokens, cols)

    def group(g, carry, i, stage):
        results = []
        for u in range(UNROLL):
            k = g * UNROLL + u
            s = stage * slots + k
            qb, cb = load_pair(s, pair_query, met_ref, masks)
            rows = kv[i, rows_at(pair_row[s], tokens)]
            expd, d_prob = pair_scores(qb, cb, rows[:, :cols], rows[:, cols:], pair_len[s])
            total = jnp.sum(expd, axis=0, keepdims=True)
            safe = jnp.where(total > 0.0, total, 1.0)
            mean = jnp.sum((expd / safe) * d_prob, axis=0, keepdims=True)
            results.append((i * slots + k, pair_query[s], total, mean))
        for k, qi, total, mean in results:
            rows_ref[pl.ds(k, 1), :] = total
            old_total, old_mean = row_of(sums, 0, qi), row_of(sums, 1, qi)
            both = old_total + total
            safe = jnp.where(both > 0.0, both, 1.0)
            sums[0, pl.ds(qi, 1), :] = both
            sums[1, pl.ds(qi, 1), :] = old_mean * (old_total / safe) + mean * (total / safe)
        return carry

    for copy in copies:
        copy.wait()
    each_group(count, stages, group)
    if last:
        for i in range(1, out_ref.shape[0]):
            out_ref[i] = out_ref[0]


def mass_kernel(query_ref, col_ref, own_ref, near_ref, opp_ref, sums_ref, *refs):
    out_ref = refs[-1]
    slots, queries, cols = query_ref.shape[0], sums_ref.shape[1], out_ref.shape[1]
    of_query = lax.broadcasted_iota(jnp.int32, (slots, queries), 1) == query_ref[...]
    of_col = lax.broadcasted_iota(jnp.int32, (slots, cols), 1) == col_ref[...]
    pick = of_query.astype(F32)
    exact = dict(precision=lax.Precision.HIGHEST, preferred_element_type=F32)
    total = jnp.dot(pick, sums_ref[0], **exact)
    rows = jnp.concatenate([own_ref[...], near_ref[...], opp_ref[...]], axis=0)
    mass = jnp.sum(rows / total, axis=1, keepdims=True)
    out_ref[...] = lax.dot_general(pick, jnp.where(of_col, mass, 0.0), TN, **exact)


def backward_kernel(stages, tokens, first, last, ordered, count, pair_query, pair_row, pair_len, met_ref, sums_in, *refs):
    n = len(stages)
    kv_refs, refs, sems = refs[: 2 * n], refs[2 * n : -1], refs[-1]
    if first:
        sums_ref = refs[2 * n + 1]
        queries = met_ref.shape[0]
        total = sums_in[0, 0, :queries]
        for i in range(1, sums_in.shape[0]):
            total = total + sums_in[i, 0, :queries]
        delta = jnp.zeros_like(total)
        for i in range(sums_in.shape[0]):
            delta = delta + sums_in[i, 1, :queries] * (sums_in[i, 0, :queries] / total)
        sums_ref[0] = total
        sums_ref[1] = delta
    else:
        sums_ref = sums_in
        old_ref, refs = refs[0], refs[1 + ordered :]
        refs[2 * n + 1][...] = jnp.zeros_like(refs[2 * n + 1])
    out_refs, ctx_ref = refs[: 2 * n], refs[2 * n]
    kv, acc = (refs[-3], refs[-2]) if last else (refs[-2], refs[-1])
    ctx = refs[-1] if last else ctx_ref
    copies = join_halves(kv_refs, kv, sems)
    slots = pair_query.shape[0] // 4
    cols = kv.shape[-1] // 2
    masks = head_masks(tokens, cols)
    acc[...] = jnp.zeros_like(acc)
    ctx[...] = jnp.zeros_like(ctx) if first else old_ref[...]

    def group(g, carry, i, stage):
        results = []
        for u in range(UNROLL):
            s = stage * slots + g * UNROLL + u
            place = rows_at(pair_row[s], tokens)
            qi = pair_query[s]
            qb, cb = load_pair(s, pair_query, met_ref, masks)
            rows = kv[i, place]
            value = rows[:, cols:]
            expd, d_prob = pair_scores(qb, cb, rows[:, :cols], value, pair_len[s])
            prob = expd / row_of(sums_ref, 0, qi)
            prob_b = prob.astype(BF16)
            d_scores = (prob * (d_prob - row_of(sums_ref, 1, qi)) * HD ** (-0.5)).astype(BF16)
            key_grad = jnp.dot(d_scores, qb, preferred_element_type=F32)
            value_grad = jnp.dot(prob_b, cb, preferred_element_type=F32)
            full = lax.dot_general(prob_b, value, TN, preferred_element_type=F32)
            part = jnp.zeros(ctx.shape[1:], F32)
            for h, m in enumerate(masks):
                part = jnp.where(m, full[h * HD : (h + 1) * HD], part)
            results.append((place, qi, key_grad, value_grad, part))
        for place, qi, key_grad, value_grad, part in results:
            acc[i, place, :cols] += key_grad
            acc[i, place, cols:] += value_grad
            ctx[qi] += part
        return carry

    for copy in copies:
        copy.wait()
    each_group(count, stages, group)
    half = acc.shape[1] // 2
    for i in range(n):
        out_refs[2 * i][...] = acc[i, :half].astype(BF16)
        out_refs[2 * i + 1][...] = acc[i, half:].astype(BF16)
    if last:
        ctx_ref[...] = ctx[...].astype(BF16)


def zero_of(mark):
    first = lax.slice(mark, (0,) * mark.ndim, (1,) * mark.ndim).reshape(())
    return jnp.minimum(jnp.abs(first.astype(F32)), 0.0)


def smem():
    return pl.BlockSpec(memory_space=pltpu.SMEM)


def hbm():
    return pl.BlockSpec(memory_space=pltpu.HBM)


def vmem():
    return pl.BlockSpec(memory_space=pltpu.VMEM)


def per_device(queries_vec, retr_query, passages, kv_weight, retrieval, lengths, ctx_cot):
    nz, ny, nx, nc = (lax.axis_size(a) for a in ("z", "y", "x", "core"))
    z, y, x, core = (lax.axis_index(a) for a in ("z", "y", "x", "core"))
    own_count, token_count, local_width = passages.shape
    full_width = kv_weight.shape[0]
    head_cols = kv_weight.shape[2]
    query_count, query_tokens, _ = queries_vec.shape
    picks = retrieval.shape[1]
    width_scale = INV_TEMP * full_width ** (-0.5)
    tokens = own_count * token_count
    half = tokens // 2
    meet_queries = nz * query_count
    meet_rows = ny * own_count
    stage_slots = 2 * nz
    cap = ny * stage_slots

    kv_cols = 2 * head_cols
    blocks = kv_weight.reshape(nx, nc, local_width, kv_cols)

    def weight_block(dx, dc):
        return blocks[(x + dx) % nx, (core + dc) % nc]

    params = pltpu.CompilerParams(vmem_limit_bytes=VMEM_LIMIT)
    cost = pl.CostEstimate(flops=1 << 30, bytes_accessed=8 << 20, transcendentals=1 << 20)

    with jax.named_scope("gather_queries"):
        packed = jnp.concatenate(
            [queries_vec, ctx_cot, retr_query.reshape(query_count, -1, head_cols)], axis=1
        )
        met = lax.all_gather(packed, "z", axis=0, tiled=True)
        rq_all = met[:, 2 * query_tokens :].reshape(meet_queries, local_width)

    with jax.named_scope("project"):
        own = passages.reshape(tokens, local_width)
        left = shift(own, "x", 1)
        right = shift(own, "x", -1)
        opp_a = shift(left[:half], "x", 1)
        opp_b = shift(right[half:], "x", -1)
        opp = jnp.concatenate([opp_a, opp_b], axis=0)
        acc = jnp.dot(own, weight_block(0, 0), preferred_element_type=F32)
        for part, dx, dc in (
            (own, 0, 1), (left, -1, 0), (right, 1, 0), (left, -1, 1), (right, 1, 1), (opp, 2, 0), (opp, 2, 1),
        ):
            part = swap(part, "core", 1) if dc else part
            acc = acc + jnp.dot(part, weight_block(dx, dc), preferred_element_type=F32)
        kv_a, kv_b = acc[:half].astype(BF16), acc[half:].astype(BF16)

    with jax.named_scope("gather_rows"):
        own = (kv_a, kv_b)
        left_a = shift(kv_a, "y", 1)
        right_b = shift(kv_b, "y", -1)
        left_b = shift(kv_b, "y", 1)
        right_a = shift(kv_a, "y", -1)
        opp = (shift(left_a, "y", 1), shift(right_b, "y", -1))
        left, right = (left_a, left_b), (right_a, right_b)

    with jax.named_scope("pool"):
        own_id = z * ny + y
        own_lengths = lax.dynamic_slice_in_dim(lengths, own_id * own_count, own_count)
        positions = jnp.arange(token_count, dtype=jnp.int32)
        own_valid = positions[None, :] < own_lengths[:, None]
        own_len_f = own_lengths.astype(F32)
        pooled = jnp.einsum("pt,ptd->pd", own_valid.astype(BF16) + zero_of(kv_a).astype(BF16), passages, preferred_element_type=F32)
        pooled = (pooled / own_len_f[:, None]).astype(BF16)
        pooled_all = jnp.concatenate([pooled] + [shift(pooled, "y", j) for j in range(1, ny)], axis=0)

    with jax.named_scope("pairs"):
        column = lax.dynamic_index_in_dim(
            retrieval.reshape(nz, ny, query_count, picks), y, axis=1, keepdims=False
        ).reshape(meet_queries * picks) + zero_of(kv_a).astype(jnp.int32)
        flat = jnp.arange(meet_queries * picks, dtype=jnp.int32)
        owner = column // own_count
        chosen = owner // ny == z
        away = (y - owner % ny) % ny
        stage_of = jnp.where(away < 2, away, 5 - away)
        same = stage_of[None, :] == stage_of[:, None]
        rank = jnp.sum((chosen[None, :] & same & (flat[None, :] < flat[:, None])).astype(jnp.int32), axis=1)
        slot_of = stage_of * stage_slots + rank
        slots = jnp.arange(cap, dtype=jnp.int32)
        hot = (slot_of[None, :] == slots[:, None]) & chosen[None, :]
        pick = lambda v: jnp.sum(jnp.where(hot, v[None, :], 0), axis=1)
        pair_query = pick(flat // picks)
        pair_id = pick(column)
        pair_row = pair_id % own_count
        filled = jnp.any(hot, axis=1)
        all_ids = jnp.arange(lengths.shape[0], dtype=jnp.int32)
        pair_len = jnp.sum(
            jnp.where((pair_id[:, None] == all_ids[None, :]) & filled[:, None], lengths[None, :], 0), axis=1
        )
        stage_ids = jnp.arange(ny, dtype=jnp.int32)
        count = jnp.sum((chosen[None, :] & (stage_of[None, :] == stage_ids[:, None])).astype(jnp.int32), axis=1)
        stage = slots // stage_slots
        slot_away = jnp.where(stage < 2, stage, 5 - stage)
        met_rows = jnp.arange(meet_rows, dtype=jnp.int32)
        met_queries = jnp.arange(meet_queries, dtype=jnp.int32)

    pairs = (count, pair_query, pair_row, pair_len)
    plane = (half, kv_cols)
    ctx_shape = (meet_queries, query_tokens, head_cols)

    def scratch(n, dtype):
        return pltpu.VMEM((n, tokens, kv_cols), dtype)

    sums_shape = (2, meet_queries, head_cols)
    sent_shape = (nz, 2, meet_queries + 8, head_cols)

    def forward(stages, *operands, last=False):
        n = len(stages)
        return pl.pallas_call(
            functools.partial(forward_kernel, stages, token_count, last),
            out_shape=(
                jax.ShapeDtypeStruct(sent_shape if last else sums_shape, F32),
                jax.ShapeDtypeStruct((n * stage_slots, head_cols), F32),
            ),
            in_specs=[smem()] * 4 + [vmem()] + [hbm()] * (2 * n) + [vmem()] * (len(operands) - 2 * n),
            out_specs=(vmem(), vmem()),
            scratch_shapes=[scratch(n, BF16), pltpu.SemaphoreType.DMA((2 * n,))],
            compiler_params=params,
            cost_estimate=cost,
        )(*pairs, met, *operands)

    def backward(stages, sums, rows, ctx=None, last=False, after=()):
        n = len(stages)
        first = ctx is None
        operands = rows if first else (*rows, ctx)
        outs = [jax.ShapeDtypeStruct(plane, BF16)] * (2 * n)
        outs += [jax.ShapeDtypeStruct(ctx_shape, BF16 if last else F32)]
        outs += [jax.ShapeDtypeStruct(sums_shape if first else (meet_queries, meet_rows), F32)]
        return pl.pallas_call(
            functools.partial(backward_kernel, stages, token_count, first, last, len(after)),
            out_shape=outs,
            in_specs=[smem()] * 4 + [vmem()] * 2 + [hbm()] * (2 * n) + [vmem()] * (len(operands) - 2 * n)
            + [pl.BlockSpec(memory_space=pl.ANY)] * len(after),
            out_specs=[vmem()] * len(outs),
            scratch_shapes=[scratch(n, BF16), scratch(n, F32)] + [pltpu.VMEM(ctx_shape, F32)] * last
            + [pltpu.SemaphoreType.DMA((2 * n,))],
            compiler_params=params,
            cost_estimate=cost,
        )(*pairs, met, sums, *operands, *after)

    with jax.named_scope("forward"):
        sums, row_own = forward((0,), *own)
        sums, row_near = forward((1, 2), *left, *right, sums)

    with jax.named_scope("scores"):
        pair_col = slot_away * own_count + pair_row
        dense = (
            (pair_query[:, None, None] == met_queries[None, :, None])
            & (pair_col[:, None, None] == met_rows[None, None, :])
            & filled[:, None, None]
        )
        is_pair = jnp.any(dense, axis=0)
        score = jnp.einsum("qd,pd->qp", rq_all, pooled_all, preferred_element_type=F32)
        score = score + swap(score, "core", 1)
        score = score + swap(score, "x", 1)
        score = (score + swap(score, "x", 2)) * width_scale
        exps = jnp.sum(jnp.where(is_pair, jnp.exp(score), 0.0), axis=1)
        exps = jnp.pad(exps[None], ((0, 0), (0, 128 - meet_queries)))

    with jax.named_scope("forward"):
        sums, row_opp = forward((3,), *opp, sums, exps, last=True)

    with jax.named_scope("exchange"):
        sums = lax.all_to_all(sums, "z", split_axis=0, concat_axis=0, tiled=True)
        log_total = jnp.log(jnp.sum(sums[:, 0, meet_queries, :meet_queries], axis=0))

    with jax.named_scope("return_rows"):
        p2_a, p2_b, ctx, sums = backward((3,), sums, opp)
        far_a = shift(p2_a, "y", 1)
        far_b = shift(p2_b, "y", -1)
        mass_part = pl.pallas_call(
            mass_kernel,
            out_shape=jax.ShapeDtypeStruct((meet_queries, meet_rows), F32),
            in_specs=[vmem()] * 6 + [pl.BlockSpec(memory_space=pl.ANY)] * 2,
            out_specs=vmem(),
            compiler_params=params,
        )(pair_query[:, None], pair_col[:, None], row_own, row_near, row_opp, sums, p2_a, p2_b)
        p3_a, p3_b, p1_a, p1_b, ctx, zeros = backward((1, 2), sums, left + right, ctx, after=(mass_part,))
        mass = mass_part + swap(mass_part, "core", 1) + zeros
        near_b = shift(p1_b, "y", 1)
        near_a = shift(p3_a, "y", -1)
        up_in = p1_a + far_a
        down_in = p3_b + far_b
        up_a = shift(up_in, "y", 1)
        down_b = shift(down_in, "y", -1)
        p0_a, p0_b, ctx, zeros = backward((0,), sums, own, ctx, True, (up_in, down_in, mass))

    with jax.named_scope("context"):
        context = lax.psum_scatter(ctx, "z", scatter_dimension=0, tiled=True)

    with jax.named_scope("return_rows"):
        add3 = lambda u, v, w: (u.astype(F32) + v.astype(F32) + w.astype(F32)).astype(BF16)
        grad_rows = jnp.concatenate([add3(p0_a, up_a, near_a), add3(p0_b, near_b, down_b)], axis=0)

    with jax.named_scope("weights_back"):
        def back(dx, dc):
            return lax.dot_general(grad_rows, weight_block(dx, dc), NT, preferred_element_type=F32)

        def both_cores(dx):
            other = swap(back(dx, 1).astype(BF16), "core", 1)
            return back(dx, 0) + other.astype(F32), other

        s2, o2 = both_cores(2)
        s1, _ = both_cores(1)
        s3, _ = both_cores(-1)
        s0, _ = both_cores(0)
        xfar_a = shift(s2[:half].astype(BF16), "x", 1)
        xfar_b = shift(s2[half:].astype(BF16), "x", -1)
        xnear_b = shift(s1[half:].astype(BF16), "x", 1)
        xnear_a = shift(s3[:half].astype(BF16), "x", -1)
        xup_a = shift((s1[:half] + xfar_a.astype(F32)).astype(BF16), "x", 1)
        xdown_b = shift((s3[half:] + xfar_b.astype(F32)).astype(BF16), "x", -1)
        reader_grad = jnp.concatenate([
            s0[:half] + xup_a.astype(F32) + xnear_a.astype(F32),
            s0[half:] + xnear_b.astype(F32) + xdown_b.astype(F32),
        ], axis=0)

    with jax.named_scope("distill"):
        mass = mass + swap(mass, "x", 1) + zeros
        mass = (mass + swap(mass, "x", 2)) / (HEADS * query_tokens)
        log_prob = score - log_total[:, None]
        later = zero_of(o2)
        d_score = jnp.where(is_pair, DISTILL * (jnp.exp(log_prob) - mass) * width_scale, 0.0)
        pool_part = jnp.einsum(
            "qp,qd->pd", d_score + later, rq_all.astype(F32), precision=lax.Precision.HIGHEST,
            preferred_element_type=F32,
        ).reshape(ny, own_count, local_width)
        grad_pool = pool_part[0]
        for j in range(1, ny):
            grad_pool = grad_pool + shift(pool_part[j], "y", -j)
        log_mass = jnp.log(jnp.where(is_pair, mass, 1.0))
        divergence = jnp.sum(jnp.where(is_pair, mass * (log_mass - log_prob), 0.0), axis=1)[None]
        for bit, pause in ((1, 0.0), (2, later), (4, 0.0)):
            divergence = divergence + pause
            divergence = divergence + swap(divergence, "z", bit)
        divergence = lax.dynamic_slice_in_dim(divergence[0], z * query_count, query_count)
        retr_grad = own_valid.astype(F32)[:, :, None] / own_len_f[:, None, None] * grad_pool[:, None, :]

    grad_passages = (reader_grad.reshape(passages.shape) + retr_grad).astype(BF16)
    return (context, divergence, grad_passages)


def solution(mesh):
    grid = Mesh(mesh.devices.reshape(8, 4, 4, 2), ("z", "y", "x", "core"))
    dp, mp = ("z", "y"), ("x", "core")
    in_specs = (
        P(dp, None, mp),
        P(dp, mp),
        P(dp, None, mp),
        P(None, None, mp),
        P(),
        P(),
        P(dp, None, mp),
    )
    out_specs = (P(dp, None, mp), P(dp), P(dp, None, mp))
    return jax.shard_map(
        per_device, mesh=grid, in_specs=in_specs, out_specs=out_specs, check_vma=False
    )
```

```python
import functools

import jax
import jax.numpy as jnp
from jax import lax
from jax.experimental import pallas as pl
from jax.experimental.pallas import tpu as pltpu
from jax.sharding import Mesh, PartitionSpec as P

HEADS = 32
HD = 64
INV_TEMP = 8.0
DISTILL = 128.0
UNROLL = 4
VMEM_LIMIT = 14 * 1024 * 1024
F32 = jnp.float32
BF16 = jnp.bfloat16
NT = (((1,), (1,)), ((), ()))
TN = (((0,), (0,)), ((), ()))


def shift(x, axis, step):
    size = lax.axis_size(axis)
    return lax.ppermute(x, axis, [(i, (i + step) % size) for i in range(size)])


def swap(x, axis, bit):
    size = lax.axis_size(axis)
    return lax.ppermute(x, axis, [(i, i ^ bit) for i in range(size)])


def head_masks(rows, cols):
    lane = lax.broadcasted_iota(jnp.int32, (rows, cols), 1)
    return [lane // HD == h for h in range(cols // HD)]


def block_diagonal(x, masks):
    zero = jnp.zeros_like(x)
    return jnp.concatenate([jnp.where(m, x, zero) for m in masks], axis=0)


def pair_scores(qb, cb, key, value, length):
    scores = lax.dot_general(key, qb, NT, preferred_element_type=F32) * HD ** (-0.5)
    d_prob = lax.dot_general(value, cb, NT, preferred_element_type=F32)
    row = lax.broadcasted_iota(jnp.int32, scores.shape, 0)
    return jnp.where(row < length, jnp.exp(scores), 0.0), d_prob


def load_pair(slot, pair_query, met_ref, masks):
    tokens = masks[0].shape[0]
    both = met_ref[pair_query[slot], : 2 * tokens]
    return block_diagonal(both[:tokens], masks), block_diagonal(both[tokens:], masks)


def join_halves(refs, scratch, sems):
    half = refs[0].shape[0]
    copies = [
        pltpu.make_async_copy(ref, scratch.at[k // 2, pl.ds((k % 2) * half, half)], sems.at[k])
        for k, ref in enumerate(refs)
    ]
    for copy in copies:
        copy.start()
    return copies


def rows_at(row, tokens):
    return pl.ds(pl.multiple_of(row * tokens, tokens), tokens)


def each_group(count, stages, body):
    for i, stage in enumerate(stages):
        groups = (count[stage] + UNROLL - 1) // UNROLL
        lax.fori_loop(0, groups, lambda g, carry: body(g, carry, i, stage), 0)


def row_of(ref, part, index):
    return ref[part, pl.ds(index, 1), :]


def forward_kernel(stages, tokens, last, count, pair_query, pair_row, pair_len, met_ref, *refs):
    n = len(stages)
    kv_refs, refs = refs[: 2 * n], refs[2 * n :]
    out_ref, rows_ref, kv, sems = refs[-4:]
    sums = out_ref.at[0] if last else out_ref
    queries = met_ref.shape[0]
    copies = join_halves(kv_refs, kv, sems)
    rows_ref[...] = jnp.zeros_like(rows_ref)
    if stages[0]:
        sums[:, :queries] = refs[0][...]
    else:
        sums[...] = jnp.zeros(sums.shape, F32)
    if last:
        sums[:, queries:] = jnp.zeros((2, sums.shape[1] - queries, sums.shape[2]), F32)
        sums[0, queries : queries + 1, : refs[1].shape[1]] = refs[1][...]
    slots = rows_ref.shape[0] // n
    cols = kv.shape[-1] // 2
    masks = head_masks(tokens, cols)

    def group(g, carry, i, stage):
        results = []
        for u in range(UNROLL):
            k = g * UNROLL + u
            s = stage * slots + k
            qb, cb = load_pair(s, pair_query, met_ref, masks)
            rows = kv[i, rows_at(pair_row[s], tokens)]
            expd, d_prob = pair_scores(qb, cb, rows[:, :cols], rows[:, cols:], pair_len[s])
            total = jnp.sum(expd, axis=0, keepdims=True)
            safe = jnp.where(total > 0.0, total, 1.0)
            mean = jnp.sum((expd / safe) * d_prob, axis=0, keepdims=True)
            results.append((i * slots + k, pair_query[s], total, mean))
        for k, qi, total, mean in results:
            rows_ref[pl.ds(k, 1), :] = total
            old_total, old_mean = row_of(sums, 0, qi), row_of(sums, 1, qi)
            both = old_total + total
            safe = jnp.where(both > 0.0, both, 1.0)
            sums[0, pl.ds(qi, 1), :] = both
            sums[1, pl.ds(qi, 1), :] = old_mean * (old_total / safe) + mean * (total / safe)
        return carry

    for copy in copies:
        copy.wait()
    each_group(count, stages, group)
    if last:
        for i in range(1, out_ref.shape[0]):
            out_ref[i] = out_ref[0]


def mass_kernel(query_ref, col_ref, own_ref, near_ref, opp_ref, sums_ref, *refs):
    out_ref = refs[-1]
    slots, queries, cols = query_ref.shape[0], sums_ref.shape[1], out_ref.shape[1]
    of_query = lax.broadcasted_iota(jnp.int32, (slots, queries), 1) == query_ref[...]
    of_col = lax.broadcasted_iota(jnp.int32, (slots, cols), 1) == col_ref[...]
    pick = of_query.astype(F32)
    exact = dict(precision=lax.Precision.HIGHEST, preferred_element_type=F32)
    total = jnp.dot(pick, sums_ref[0], **exact)
    rows = jnp.concatenate([own_ref[...], near_ref[...], opp_ref[...]], axis=0)
    mass = jnp.sum(rows / total, axis=1, keepdims=True)
    out_ref[...] = lax.dot_general(pick, jnp.where(of_col, mass, 0.0), TN, **exact)


def backward_kernel(stages, tokens, first, last, ordered, count, pair_query, pair_row, pair_len, met_ref, sums_in, *refs):
    n = len(stages)
    kv_refs, refs, sems = refs[: 2 * n], refs[2 * n : -1], refs[-1]
    if first:
        sums_ref = refs[2 * n + 1]
        queries = met_ref.shape[0]
        total = sums_in[0, 0, :queries]
        for i in range(1, sums_in.shape[0]):
            total = total + sums_in[i, 0, :queries]
        delta = jnp.zeros_like(total)
        for i in range(sums_in.shape[0]):
            delta = delta + sums_in[i, 1, :queries] * (sums_in[i, 0, :queries] / total)
        sums_ref[0] = total
        sums_ref[1] = delta
    else:
        sums_ref = sums_in
        old_ref, refs = refs[0], refs[1 + ordered :]
        refs[2 * n + 1][...] = jnp.zeros_like(refs[2 * n + 1])
    out_refs, ctx_ref = refs[: 2 * n], refs[2 * n]
    kv, acc = (refs[-3], refs[-2]) if last else (refs[-2], refs[-1])
    ctx = refs[-1] if last else ctx_ref
    copies = join_halves(kv_refs, kv, sems)
    slots = pair_query.shape[0] // 4
    cols = kv.shape[-1] // 2
    masks = head_masks(tokens, cols)
    acc[...] = jnp.zeros_like(acc)
    ctx[...] = jnp.zeros_like(ctx) if first else old_ref[...]

    def group(g, carry, i, stage):
        results = []
        for u in range(UNROLL):
            s = stage * slots + g * UNROLL + u
            place = rows_at(pair_row[s], tokens)
            qi = pair_query[s]
            qb, cb = load_pair(s, pair_query, met_ref, masks)
            rows = kv[i, place]
            value = rows[:, cols:]
            expd, d_prob = pair_scores(qb, cb, rows[:, :cols], value, pair_len[s])
            prob = expd / row_of(sums_ref, 0, qi)
            prob_b = prob.astype(BF16)
            d_scores = (prob * (d_prob - row_of(sums_ref, 1, qi)) * HD ** (-0.5)).astype(BF16)
            key_grad = jnp.dot(d_scores, qb, preferred_element_type=F32)
            value_grad = jnp.dot(prob_b, cb, preferred_element_type=F32)
            full = lax.dot_general(prob_b, value, TN, preferred_element_type=F32)
            part = jnp.zeros(ctx.shape[1:], F32)
            for h, m in enumerate(masks):
                part = jnp.where(m, full[h * HD : (h + 1) * HD], part)
            results.append((place, qi, key_grad, value_grad, part))
        for place, qi, key_grad, value_grad, part in results:
            acc[i, place, :cols] += key_grad
            acc[i, place, cols:] += value_grad
            ctx[qi] += part
        return carry

    for copy in copies:
        copy.wait()
    each_group(count, stages, group)
    half = acc.shape[1] // 2
    for i in range(n):
        out_refs[2 * i][...] = acc[i, :half].astype(BF16)
        out_refs[2 * i + 1][...] = acc[i, half:].astype(BF16)
    if last:
        ctx_ref[...] = ctx[...].astype(BF16)


def zero_of(mark):
    first = lax.slice(mark, (0,) * mark.ndim, (1,) * mark.ndim).reshape(())
    return jnp.minimum(jnp.abs(first.astype(F32)), 0.0)


def smem():
    return pl.BlockSpec(memory_space=pltpu.SMEM)


def hbm():
    return pl.BlockSpec(memory_space=pltpu.HBM)


def vmem():
    return pl.BlockSpec(memory_space=pltpu.VMEM)


def per_device(queries_vec, retr_query, passages, kv_weight, retrieval, lengths, ctx_cot):
    nz, ny, nx, nc = (lax.axis_size(a) for a in ("z", "y", "x", "core"))
    z, y, x, core = (lax.axis_index(a) for a in ("z", "y", "x", "core"))
    own_count, token_count, local_width = passages.shape
    full_width = kv_weight.shape[0]
    head_cols = kv_weight.shape[2]
    query_count, query_tokens, _ = queries_vec.shape
    picks = retrieval.shape[1]
    width_scale = INV_TEMP * full_width ** (-0.5)
    tokens = own_count * token_count
    half = tokens // 2
    meet_queries = nz * query_count
    meet_rows = ny * own_count
    stage_slots = 2 * nz
    cap = ny * stage_slots

    kv_cols = 2 * head_cols
    blocks = kv_weight.reshape(nx, nc, local_width, kv_cols)

    def weight_block(dx, dc):
        return blocks[(x + dx) % nx, (core + dc) % nc]

    params = pltpu.CompilerParams(vmem_limit_bytes=VMEM_LIMIT)
    cost = pl.CostEstimate(flops=1 << 30, bytes_accessed=8 << 20, transcendentals=1 << 20)

    with jax.named_scope("gather_queries"):
        packed = jnp.concatenate(
            [queries_vec, ctx_cot, retr_query.reshape(query_count, -1, head_cols)], axis=1
        )
        met = lax.all_gather(packed, "z", axis=0, tiled=True)
        rq_all = met[:, 2 * query_tokens :].reshape(meet_queries, local_width)

    with jax.named_scope("project"):
        own = passages.reshape(tokens, local_width)
        left = shift(own, "x", 1)
        right = shift(own, "x", -1)
        opp_a = shift(left[:half], "x", 1)
        opp_b = shift(right[half:], "x", -1)
        opp = jnp.concatenate([opp_a, opp_b], axis=0)
        acc = jnp.dot(own, weight_block(0, 0), preferred_element_type=F32)
        for part, dx, dc in (
            (own, 0, 1), (left, -1, 0), (right, 1, 0), (left, -1, 1), (right, 1, 1), (opp, 2, 0), (opp, 2, 1),
        ):
            part = swap(part, "core", 1) if dc else part
            acc = acc + jnp.dot(part, weight_block(dx, dc), preferred_element_type=F32)
        kv_a, kv_b = acc[:half].astype(BF16), acc[half:].astype(BF16)

    with jax.named_scope("gather_rows"):
        own = (kv_a, kv_b)
        left_a = shift(kv_a, "y", 1)
        right_b = shift(kv_b, "y", -1)
        left_b = shift(kv_b, "y", 1)
        right_a = shift(kv_a, "y", -1)
        opp = (shift(left_a, "y", 1), shift(right_b, "y", -1))
        left, right = (left_a, left_b), (right_a, right_b)

    with jax.named_scope("pool"):
        own_id = z * ny + y
        own_lengths = lax.dynamic_slice_in_dim(lengths, own_id * own_count, own_count)
        positions = jnp.arange(token_count, dtype=jnp.int32)
        own_valid = positions[None, :] < own_lengths[:, None]
        own_len_f = own_lengths.astype(F32)
        pooled = jnp.einsum("pt,ptd->pd", own_valid.astype(BF16) + zero_of(kv_a).astype(BF16), passages, preferred_element_type=F32)
        pooled = (pooled / own_len_f[:, None]).astype(BF16)
        pooled_all = jnp.concatenate([pooled] + [shift(pooled, "y", j) for j in range(1, ny)], axis=0)

    with jax.named_scope("pairs"):
        column = lax.dynamic_index_in_dim(
            retrieval.reshape(nz, ny, query_count, picks), y, axis=1, keepdims=False
        ).reshape(meet_queries * picks) + zero_of(kv_a).astype(jnp.int32)
        flat = jnp.arange(meet_queries * picks, dtype=jnp.int32)
        owner = column // own_count
        chosen = owner // ny == z
        away = (y - owner % ny) % ny
        stage_of = jnp.where(away < 2, away, 5 - away)
        same = stage_of[None, :] == stage_of[:, None]
        rank = jnp.sum((chosen[None, :] & same & (flat[None, :] < flat[:, None])).astype(jnp.int32), axis=1)
        slot_of = stage_of * stage_slots + rank
        slots = jnp.arange(cap, dtype=jnp.int32)
        hot = (slot_of[None, :] == slots[:, None]) & chosen[None, :]
        pick = lambda v: jnp.sum(jnp.where(hot, v[None, :], 0), axis=1)
        pair_query = pick(flat // picks)
        pair_id = pick(column)
        pair_row = pair_id % own_count
        filled = jnp.any(hot, axis=1)
        all_ids = jnp.arange(lengths.shape[0], dtype=jnp.int32)
        pair_len = jnp.sum(
            jnp.where((pair_id[:, None] == all_ids[None, :]) & filled[:, None], lengths[None, :], 0), axis=1
        )
        stage_ids = jnp.arange(ny, dtype=jnp.int32)
        count = jnp.sum((chosen[None, :] & (stage_of[None, :] == stage_ids[:, None])).astype(jnp.int32), axis=1)
        stage = slots // stage_slots
        slot_away = jnp.where(stage < 2, stage, 5 - stage)
        met_rows = jnp.arange(meet_rows, dtype=jnp.int32)
        met_queries = jnp.arange(meet_queries, dtype=jnp.int32)

    pairs = (count, pair_query, pair_row, pair_len)
    plane = (half, kv_cols)
    ctx_shape = (meet_queries, query_tokens, head_cols)

    def scratch(n, dtype):
        return pltpu.VMEM((n, tokens, kv_cols), dtype)

    sums_shape = (2, meet_queries, head_cols)
    sent_shape = (nz, 2, meet_queries + 8, head_cols)

    def forward(stages, *operands, last=False):
        n = len(stages)
        return pl.pallas_call(
            functools.partial(forward_kernel, stages, token_count, last),
            out_shape=(
                jax.ShapeDtypeStruct(sent_shape if last else sums_shape, F32),
                jax.ShapeDtypeStruct((n * stage_slots, head_cols), F32),
            ),
            in_specs=[smem()] * 4 + [vmem()] + [hbm()] * (2 * n) + [vmem()] * (len(operands) - 2 * n),
            out_specs=(vmem(), vmem()),
            scratch_shapes=[scratch(n, BF16), pltpu.SemaphoreType.DMA((2 * n,))],
            compiler_params=params,
            cost_estimate=cost,
        )(*pairs, met, *operands)

    def backward(stages, sums, rows, ctx=None, last=False, after=()):
        n = len(stages)
        first = ctx is None
        operands = rows if first else (*rows, ctx)
        outs = [jax.ShapeDtypeStruct(plane, BF16)] * (2 * n)
        outs += [jax.ShapeDtypeStruct(ctx_shape, BF16 if last else F32)]
        outs += [jax.ShapeDtypeStruct(sums_shape if first else (meet_queries, meet_rows), F32)]
        return pl.pallas_call(
            functools.partial(backward_kernel, stages, token_count, first, last, len(after)),
            out_shape=outs,
            in_specs=[smem()] * 4 + [vmem()] * 2 + [hbm()] * (2 * n) + [vmem()] * (len(operands) - 2 * n)
            + [pl.BlockSpec(memory_space=pl.ANY)] * len(after),
            out_specs=[vmem()] * len(outs),
            scratch_shapes=[scratch(n, BF16), scratch(n, F32)] + [pltpu.VMEM(ctx_shape, F32)] * last
            + [pltpu.SemaphoreType.DMA((2 * n,))],
            compiler_params=params,
            cost_estimate=cost,
        )(*pairs, met, sums, *operands, *after)

    with jax.named_scope("forward"):
        sums, row_own = forward((0,), *own)
        sums, row_near = forward((1, 2), *left, *right, sums)

    with jax.named_scope("scores"):
        pair_col = slot_away * own_count + pair_row
        dense = (
            (pair_query[:, None, None] == met_queries[None, :, None])
            & (pair_col[:, None, None] == met_rows[None, None, :])
            & filled[:, None, None]
        )
        is_pair = jnp.any(dense, axis=0)
        score = jnp.einsum("qd,pd->qp", rq_all, pooled_all, preferred_element_type=F32)
        score = score + swap(score, "core", 1)
        score = score + swap(score, "x", 1)
        score = (score + swap(score, "x", 2)) * width_scale
        exps = jnp.sum(jnp.where(is_pair, jnp.exp(score), 0.0), axis=1)
        exps = jnp.pad(exps[None], ((0, 0), (0, 128 - meet_queries)))

    with jax.named_scope("forward"):
        sums, row_opp = forward((3,), *opp, sums, exps, last=True)

    with jax.named_scope("exchange"):
        sums = lax.all_to_all(sums, "z", split_axis=0, concat_axis=0, tiled=True)
        log_total = jnp.log(jnp.sum(sums[:, 0, meet_queries, :meet_queries], axis=0))

    with jax.named_scope("return_rows"):
        p2_a, p2_b, ctx, sums = backward((3,), sums, opp)
        far_a = shift(p2_a, "y", 1)
        far_b = shift(p2_b, "y", -1)
        mass_part = pl.pallas_call(
            mass_kernel,
            out_shape=jax.ShapeDtypeStruct((meet_queries, meet_rows), F32),
            in_specs=[vmem()] * 6 + [pl.BlockSpec(memory_space=pl.ANY)] * 2,
            out_specs=vmem(),
            compiler_params=params,
        )(pair_query[:, None], pair_col[:, None], row_own, row_near, row_opp, sums, p2_a, p2_b)
        p3_a, p3_b, p1_a, p1_b, ctx, zeros = backward((1, 2), sums, left + right, ctx, after=(mass_part,))
        mass = mass_part + swap(mass_part, "core", 1) + zeros
        near_b = shift(p1_b, "y", 1)
        near_a = shift(p3_a, "y", -1)
        up_in = p1_a + far_a
        down_in = p3_b + far_b
        up_a = shift(up_in, "y", 1)
        down_b = shift(down_in, "y", -1)
        p0_a, p0_b, ctx, zeros = backward((0,), sums, own, ctx, True, (up_in, down_in, mass))

    with jax.named_scope("context"):
        context = lax.psum_scatter(ctx, "z", scatter_dimension=0, tiled=True)

    with jax.named_scope("return_rows"):
        add3 = lambda u, v, w: (u.astype(F32) + v.astype(F32) + w.astype(F32)).astype(BF16)
        grad_rows = jnp.concatenate([add3(p0_a, up_a, near_a), add3(p0_b, near_b, down_b)], axis=0)

    with jax.named_scope("weights_back"):
        def back(dx, dc):
            return lax.dot_general(grad_rows, weight_block(dx, dc), NT, preferred_element_type=F32)

        def both_cores(dx):
            other = swap(back(dx, 1).astype(BF16), "core", 1)
            return back(dx, 0) + other.astype(F32), other

        s2, o2 = both_cores(2)
        s1, _ = both_cores(1)
        s3, _ = both_cores(-1)
        s0, _ = both_cores(0)
        xfar_a = shift(s2[:half].astype(BF16), "x", 1)
        xfar_b = shift(s2[half:].astype(BF16), "x", -1)
        xnear_b = shift(s1[half:].astype(BF16), "x", 1)
        xnear_a = shift(s3[:half].astype(BF16), "x", -1)
        xup_in = (s1[:half] + xfar_a.astype(F32)).astype(BF16)
        xup_a = shift(xup_in, "x", 1)
        xdown_b = shift((s3[half:] + xfar_b.astype(F32)).astype(BF16), "x", -1)
        reader_grad = jnp.concatenate([
            s0[:half] + xup_a.astype(F32) + xnear_a.astype(F32),
            s0[half:] + xnear_b.astype(F32) + xdown_b.astype(F32),
        ], axis=0)

    with jax.named_scope("distill"):
        mass = mass + swap(mass, "x", 1) + zeros
        mass = (mass + swap(mass, "x", 2)) / (HEADS * query_tokens)
        log_prob = score - log_total[:, None]
        later = zero_of(o2)
        d_score = jnp.where(is_pair, DISTILL * (jnp.exp(log_prob) - mass) * width_scale, 0.0)
        pool_part = jnp.einsum(
            "qp,qd->pd", d_score + later, rq_all.astype(F32), precision=lax.Precision.HIGHEST,
            preferred_element_type=F32,
        ).reshape(ny, own_count, local_width)
        grad_pool = pool_part[0]
        for j in range(1, ny):
            grad_pool = grad_pool + shift(pool_part[j], "y", -j)
        log_mass = jnp.log(jnp.where(is_pair, mass, 1.0))
        divergence = jnp.sum(jnp.where(is_pair, mass * (log_mass - log_prob), 0.0), axis=1)[None]
        for bit, pause in ((1, 0.0), (2, later), (4, zero_of(xup_in))):
            divergence = divergence + pause
            divergence = divergence + swap(divergence, "z", bit)
        divergence = lax.dynamic_slice_in_dim(divergence[0], z * query_count, query_count)
        retr_grad = own_valid.astype(F32)[:, :, None] / own_len_f[:, None, None] * grad_pool[:, None, :]

    grad_passages = (reader_grad.reshape(passages.shape) + retr_grad).astype(BF16)
    return (context, divergence, grad_passages)


def solution(mesh):
    grid = Mesh(mesh.devices.reshape(8, 4, 4, 2), ("z", "y", "x", "core"))
    dp, mp = ("z", "y"), ("x", "core")
    in_specs = (
        P(dp, None, mp),
        P(dp, mp),
        P(dp, None, mp),
        P(None, None, mp),
        P(),
        P(),
        P(dp, None, mp),
    )
    out_specs = (P(dp, None, mp), P(dp), P(dp, None, mp))
    return jax.shard_map(
        per_device, mesh=grid, in_specs=in_specs, out_specs=out_specs, check_vma=False
    )
```
